128 devices in a mesh: expert: 64 (over z, y, x), token: 2 (over core).
Axes of the slice: x: 4, y: 4, z: 4, core: 2. Of those that a mesh axis runs over, the one named last changes fastest.
Arguments:
- tokens: bfloat16 [4096, 3584], P('expert', 'token'), may hold values from -6 to 6
- routes: int32 [4096, 8], P('expert'), may hold values from 0 to 63, all different within a row; in each aligned block of 64 rows (0 to 63, 64 to 127, ...) at most 16 rows name the same one
- mixing: float32 [4096, 8], P('expert'), may hold values from 0.05 to 1
- gate_weight: bfloat16 [64, 3584, 1024], P('expert', None, 'token'), may hold values from -0.09375 to 0.09375
- up_weight: bfloat16 [64, 3584, 1024], P('expert', None, 'token'), may hold values from -0.09375 to 0.09375
- down_weight: bfloat16 [64, 1024, 3584], P('expert', None, 'token'), may hold values from -0.1875 to 0.1875
Outputs:
- mixed: bfloat16 [4096, 3584], P('expert', 'token')
- hessian: float32 [64, 1024, 1024], P('expert', 'token')
The draws below stay inside these ranges and needn't reach their ends.
Inputs may be any that keep to these rules, and one draw needn't show every extreme that they name: `routes`: each row names 8 different experts; among the 64 rows of one device no expert is named by more than 16 rows, and on some device an expert is named by exactly 16 rows; every expert is named by some row.
All inputs are finite; a program needn't handle non-finite values.
Results may differ from the reference program's by a relative error of at most 0.0058.
Values may be sent and summed in bfloat16 or wider, within the bound.
No kernel may reach another device: no remote copies, remote signals or barrier semaphores. Data moves between devices by JAX's collectives and lax.ppermute only.
A program may use at most 128 MiB of HBM per device.

```python
import math
import jax
import jax.numpy as jnp
import numpy as np
from jax import lax

D = 3584
FF = 1024
TOPK = 8
TOK_E = 64
EXPERTS = 64
TOKENS = 4096
CAP = 16
N_EXPERT = 64


def shard_levels(stream_key, shape, pieces, least, largest):
    gain = 1.0
    for dim, shards_of in pieces:
        draws = jax.random.uniform(jax.random.fold_in(jax.random.fold_in(stream_key, 6), dim), (shards_of,), jnp.float32, least / len(pieces), largest / len(pieces))
        gain = gain * jnp.repeat(jnp.exp(draws), shape[dim] // shards_of).reshape((-1,) + (1,) * (len(shape) - 1 - dim))
    return gain


def shared_out(own_key, own, number, rows, amount, top, reach, slope):
    ranking = jax.random.permutation(own_key, amount)
    heavy_load, common = load_shares(amount, rows * top, reach, slope, True), load_shares(amount, rows * top, reach, slope, False)
    places = jnp.arange(amount)

    def named(sizes, rotation):
        used = int((sizes > 0).sum())
        fixed = max(1, used // 4)
        shifted = fixed + (places - fixed + rotation * (used - fixed)) % max(1, amount - fixed)
        return jnp.zeros((amount,), jnp.int32).at[ranking[jnp.where(places < fixed, places, shifted)]].set(jnp.asarray(sizes, jnp.int32))

    sizes = jnp.where(number % 4 == 0, named(heavy_load, number // 4), named(common, number - number // 4 - 1))
    mixed = jax.random.permutation(jax.random.fold_in(own, 3), amount)
    giver, taker = mixed[0:amount // 2 * 2:2], mixed[1:amount // 2 * 2:2]
    margin = jnp.minimum(sizes[giver] - 1, reach - sizes[taker]) // 2
    margin = jnp.where((giver == ranking[0]) | (taker == ranking[0]) | (sizes[taker] == 0), 0, jnp.maximum(margin, 0))
    shifted = jax.random.randint(jax.random.fold_in(own, 4), (amount // 2,), 0, 1 << 20) % (margin + 1)
    sizes = sizes.at[giver].add(-shifted).at[taker].add(shifted)
    members = jnp.searchsorted(jnp.cumsum(sizes), jnp.arange(rows * top), side="right").astype(jnp.int32)
    table = members.reshape(top, rows).T
    table = table[jax.random.permutation(jax.random.fold_in(own, 1), rows)]
    rotation = jax.random.randint(jax.random.fold_in(own, 2), (rows, 1), 0, top)
    return jnp.take_along_axis(table, (jnp.arange(top)[None, :] + rotation) % top, axis=1)


def load_shares(number_of, total, bound, lean, full):
    portions = [(1 << 20) // math.isqrt(rank ** lean) + 1 for rank in range(1, number_of + 1)]
    largest = bound if full else min(bound, max(-(-total // number_of), total * portions[0] // sum(portions)))
    least = 1 if total - largest >= number_of - 1 else 0
    given, surplus = [largest] + [least] * (number_of - 1), total - largest - least * (number_of - 1)
    while surplus > 0:
        candidates = [i for i in range(1, number_of) if given[i] < largest] or [i for i in range(1, number_of) if given[i] < bound]
        whole, remaining = sum([portions[i] for i in candidates]), surplus
        for i in candidates:
            addition = min(bound - given[i], max(1, remaining * portions[i] // whole), surplus)
            given[i] = given[i] + addition
            surplus = surplus - addition
    return np.array(given)


def scatter_about(own_key, dims, deviation, limit, split=(), kind=jnp.bfloat16):
    values = deviation * jax.random.normal(own_key, dims, jnp.float32)
    if split:
        values = values * shard_levels(own_key, dims, split, -0.22, 0.18)
    return jnp.clip(values, -limit, limit).astype(kind)


def setup_inputs(seed: int = 0) -> dict:
    splits = jax.random.split(jax.random.key(seed), 7)
    tokens = scatter_about(splits[0], (TOKENS, D), 1.0, 6.0, ((0, 64), (1, 2)))
    routes_keys = jax.random.split(jax.random.fold_in(splits[1], 1), TOKENS // TOK_E)
    routes_turns = jax.random.permutation(jax.random.fold_in(splits[1], 3), TOKENS // TOK_E)
    routes = jax.vmap(lambda own, number: shared_out(jax.random.fold_in(splits[1], 2), own, number, TOK_E, EXPERTS, TOPK, CAP, 2))(routes_keys, routes_turns).reshape((TOKENS, TOPK))
    mixing = jnp.clip(jnp.exp(math.log(1.0) - 2.9957323 * jax.random.uniform(splits[2], (TOKENS, TOPK), jnp.float32) ** shard_levels(splits[2], (TOKENS, TOPK), ((0, 64),), -0.2, 0.2)), 0.05, 1.0)
    gate_weight = scatter_about(splits[3], (EXPERTS, D, FF), D ** -0.5, 0.09375, ((0, 64), (2, 2)))
    up_weight = scatter_about(splits[4], (EXPERTS, D, FF), D ** -0.5, 0.09375, ((0, 64), (2, 2)))
    down_weight = scatter_about(splits[5], (EXPERTS, FF, D), FF ** -0.5, 0.1875, ((0, 64), (2, 2)))
    return {"tokens": tokens, "routes": routes, "mixing": mixing, "gate_weight": gate_weight, "up_weight": up_weight, "down_weight": down_weight}


def reference(tokens, routes, mixing, gate_weight, up_weight, down_weight):
    tok_count = routes.shape[0]
    top_count = routes.shape[1]
    expert_count = gate_weight.shape[0]
    most_rows = N_EXPERT * CAP
    flat_ids = routes.reshape(-1).astype(jnp.int32)
    order = jnp.argsort(flat_ids, stable=True).astype(jnp.int32)
    counts = jnp.sum((flat_ids[:, None] == jnp.arange(expert_count, dtype=jnp.int32)[None, :]).astype(jnp.int32), 0)
    offsets = (jnp.cumsum(counts) - counts).astype(jnp.int32)
    padded = jnp.concatenate([order, jnp.zeros((most_rows,), jnp.int32)])

    def one_expert(index):
        picked = lax.dynamic_slice(padded, (offsets[index],), (most_rows,))
        valid = jnp.arange(most_rows, dtype=jnp.int32) < counts[index]
        rows = jnp.where(valid[:, None], tokens[picked // top_count], jnp.zeros((), tokens.dtype))
        gate = jnp.dot(rows, gate_weight[index], preferred_element_type=jnp.float32)
        upper = jnp.dot(rows, up_weight[index], preferred_element_type=jnp.float32)
        hidden = (jax.nn.silu(gate) * upper).astype(jnp.bfloat16)
        result = jnp.dot(hidden, down_weight[index], preferred_element_type=jnp.float32).astype(jnp.bfloat16)
        gram = jnp.dot(hidden.T, hidden, preferred_element_type=jnp.float32)
        return result, (2.0 / counts[index].astype(jnp.float32)) * gram

    outputs, hessian = lax.map(one_expert, jnp.arange(expert_count, dtype=jnp.int32))
    inverse = jnp.zeros(flat_ids.shape, jnp.int32).at[order].set(jnp.arange(flat_ids.shape[0], dtype=jnp.int32))
    position = (inverse - offsets[flat_ids]).astype(jnp.int32)
    gathered = outputs[flat_ids, position].reshape(tok_count, top_count, -1)
    mixed = jnp.sum(gathered.astype(jnp.float32) * mixing[:, :, None], 1).astype(jnp.bfloat16)
    return mixed, hessian
```

```python
import jax
import jax.numpy as jnp
from jax import lax
from jax.experimental import pallas as pl
from jax.experimental.pallas import tpu as pltpu
from jax.sharding import PartitionSpec as P

EMPTY = 64.0


def expert_kernel(
    core_ref, x_hbm, gate_own, up_own, gate_other, up_other, down_own, down_other,
    out_ref, hid_ref, count_ref, x, weights, downs, x_sem, w_sem, d_sem,
):
    core = core_ref[0]
    rows = x.shape[1]
    half = x.shape[2]
    ff_half = gate_own.shape[2]
    tile = weights.shape[3]
    tiles = ff_half // tile
    copies = []
    for f in range(2):
        copy = pltpu.make_async_copy(x_hbm.at[f], x.at[f], x_sem.at[f])
        copy.start()
        copies.append(copy)
    loads = []
    for side, pair in enumerate(((gate_own, up_own), (gate_other, up_other))):
        for j in range(tiles):
            for which, src in enumerate(pair):
                place = (side * tiles + j) * 2 + which
                copy = pltpu.make_async_copy(
                    src.at[0, :, pl.ds(j * tile, tile)], weights.at[place // 2, which], w_sem.at[place]
                )
                copy.start()
                loads.append(copy)
    down_loads = []
    for side, src in enumerate((down_own, down_other)):
        copy = pltpu.make_async_copy(src.at[0], downs.at[side], d_sem.at[side])
        copy.start()
        down_loads.append(copy)
    for copy in copies:
        copy.wait()
    valid = x[0, :, :128].astype(jnp.float32)[:, :1] < EMPTY / 2
    count_ref[...] = jnp.full(count_ref.shape, jnp.sum(valid.astype(jnp.float32)))

    def product(place, which):
        return jnp.dot(
            x[0], weights[place, which, :half], preferred_element_type=jnp.float32
        ) + jnp.dot(x[1], weights[place, which, half:], preferred_element_type=jnp.float32)

    for side in range(2):
        base = (core if side == 0 else 1 - core) * ff_half
        for j in range(tiles):
            place = side * tiles + j
            loads[2 * place].wait()
            loads[2 * place + 1].wait()
            gate = product(place, 0)
            upper = product(place, 1)
            hidden = jnp.where(valid, gate / (1.0 + jnp.exp(-gate)) * upper, 0.0)
            columns = pl.ds(pl.multiple_of(base + j * tile, tile), tile)
            hid_ref[:, columns] = hidden.astype(hid_ref.dtype)
    wide = 256
    for side in range(2):
        down_loads[side].wait()
        target = core if side == 0 else 1 - core
        for n in range(half // wide):
            columns = pl.ds(n * wide, wide)
            out_ref[target, :, columns] = jnp.dot(
                hid_ref[...], downs[side, :, columns], preferred_element_type=jnp.float32
            ).astype(out_ref.dtype)


def run_experts(core, x, gate_own, up_own, gate_other, up_other, down_own, down_other):
    _, rows, half = x.shape
    width = 2 * half
    ff_half = gate_own.shape[2]
    ff = 2 * ff_half
    tile = 256
    places = 2 * (ff_half // tile)
    anywhere = pl.BlockSpec(memory_space=pl.ANY)
    whole = pl.BlockSpec(memory_space=pltpu.VMEM)
    return pl.pallas_call(
        expert_kernel,
        out_shape=(
            jax.ShapeDtypeStruct((2, rows, half), jnp.bfloat16),
            jax.ShapeDtypeStruct((rows, ff), jnp.bfloat16),
            jax.ShapeDtypeStruct((8, 128), jnp.float32),
        ),
        in_specs=[pl.BlockSpec(memory_space=pltpu.SMEM)] + [anywhere] * 7,
        out_specs=(whole, whole, whole),
        scratch_shapes=[
            pltpu.VMEM((2, rows, half), jnp.bfloat16),
            pltpu.VMEM((places, 2, width, tile), jnp.bfloat16),
            pltpu.VMEM((2, ff, half), jnp.bfloat16),
            pltpu.SemaphoreType.DMA((2,)),
            pltpu.SemaphoreType.DMA((2 * places,)),
            pltpu.SemaphoreType.DMA((2,)),
        ],
        compiler_params=pltpu.CompilerParams(vmem_limit_bytes=48 * 1024 * 1024),
        cost_estimate=pl.CostEstimate(
            flops=2 * rows * width * ff * 3, bytes_accessed=6 * width * ff + 4 * rows * width,
            transcendentals=rows * ff,
        ),
    )(core, x, gate_own, up_own, gate_other, up_other, down_own, down_other)


def swap(array):
    return lax.ppermute(array, "token", [(0, 1), (1, 0)])


def shards(tokens, routes, mixing, gate_weight, up_weight, down_weight):
    tok_rows, half = tokens.shape
    experts = lax.axis_size("expert")
    capacity = 2 * tok_rows * routes.shape[1] // experts
    part = capacity // 2
    core = lax.axis_index("token")
    names = jnp.arange(experts, dtype=jnp.int32)
    match = routes.T[None, :, :] == names[:, None, None]
    chosen = jnp.any(match, axis=1)
    weight = jnp.sum(jnp.where(match, mixing.T[None], 0.0), axis=1)
    spots = jnp.arange(tok_rows, dtype=jnp.int32)
    before = (spots[:, None] < spots[None, :]).astype(jnp.bfloat16)
    rank = jnp.dot(chosen.astype(jnp.bfloat16), before, preferred_element_type=jnp.float32)
    key = jnp.where(chosen, rank.astype(jnp.int32), -1)
    counts = jnp.sum(chosen.astype(jnp.int32), axis=1)
    slot = jnp.arange(capacity, dtype=jnp.int32).reshape(2, 1, part)
    place = key[None, :, None, :] == slot[..., None]
    empty = (slot >= counts[None, :, None]).reshape(-1, 1)
    placing = place.astype(jnp.bfloat16).reshape(-1, tok_rows)
    mark = jnp.where(empty & (jnp.arange(half)[None, :] == 0), EMPTY, 0.0)
    outgoing = jnp.dot(placing, tokens, preferred_element_type=jnp.float32) + mark
    outgoing = outgoing.astype(jnp.bfloat16).reshape(2 * experts, part, half)
    received = lax.all_to_all(outgoing, ("token", "expert"), 0, 0, tiled=True)
    x = received.reshape(2, experts * part, half)
    gate_other, up_other, down_other = swap(gate_weight), swap(up_weight), swap(down_weight)
    out, hidden, count = run_experts(
        core.reshape(1), x, gate_weight, up_weight, gate_other, up_other, down_weight, down_other
    )
    returned = lax.all_to_all(
        out.reshape(2 * experts, part, half), ("token", "expert"), 0, 0, tiled=True
    ).reshape(-1, half)
    hidden_other, count_other = swap(hidden), swap(count)
    ff_half = gate_weight.shape[2]

    def outer(array):
        own = lax.dynamic_slice_in_dim(array, core * ff_half, ff_half, 1)
        return lax.dot_general(
            own, array, (((0,), (0,)), ((), ())), preferred_element_type=jnp.float32
        )

    total = count[0, 0] + count_other[0, 0]
    hessian = (2.0 / total * (outer(hidden) + outer(hidden_other)))[None]
    mixes = jnp.where(place, weight[None, :, None, :], 0.0).reshape(-1, tok_rows)
    high = lax.reduce_precision(mixes, 8, 7)
    mixes = jnp.concatenate([high, mixes - high], axis=1).astype(jnp.bfloat16)
    mixed = lax.dot_general(
        mixes, returned, (((0,), (0,)), ((), ())), preferred_element_type=jnp.float32
    )
    mixed = (mixed[:tok_rows] + mixed[tok_rows:]).astype(jnp.bfloat16)
    return mixed, hessian


def solution(mesh):
    placed = (
        P("expert", "token"),
        P("expert", None),
        P("expert", None),
        P("expert", None, "token"),
        P("expert", None, "token"),
        P("expert", None, "token"),
    )
    return jax.shard_map(
        shards,
        mesh=mesh,
        in_specs=placed,
        out_specs=(P("expert", "token"), P("expert", "token", None)),
        check_vma=False,
    )
```

```python
import functools

import jax
import jax.numpy as jnp
from jax import lax
from jax.experimental import pallas as pl
from jax.experimental.pallas import tpu as pltpu
from jax.sharding import PartitionSpec as P

EMPTY = 64.0
LOOKAHEAD = 4
VMEM_LIMIT = 61 * 1024 * 1024


def route_kernel(experts, part, wide, routes_ref, tokens_ref, out_hbm, out, sems):
    tok_rows, half = tokens_ref.shape
    steps = half // wide
    names = lax.broadcasted_iota(jnp.int32, (experts, tok_rows), 0)
    chosen = names == routes_ref[0:1, :]
    for k in range(1, routes_ref.shape[0]):
        chosen = chosen | (names == routes_ref[k : k + 1, :])
    first = lax.broadcasted_iota(jnp.int32, (tok_rows, tok_rows), 0)
    second = lax.broadcasted_iota(jnp.int32, (tok_rows, tok_rows), 1)
    rank = jnp.dot(
        chosen.astype(jnp.bfloat16), (first < second).astype(jnp.bfloat16),
        preferred_element_type=jnp.float32,
    )
    key = jnp.where(chosen, rank, -1.0)
    ones = jnp.ones((tok_rows, 128), jnp.bfloat16)
    rows = experts * part
    lane = lax.broadcasted_iota(jnp.int32, (rows, wide), 1)
    slot = lax.broadcasted_iota(jnp.int32, (experts, part, tok_rows), 1).astype(jnp.float32)
    copies = []
    for c in range(2):
        place = jnp.where(key[:, None, :] == slot + float(c * part), 1.0, 0.0)
        place = place.reshape(rows, tok_rows).astype(jnp.bfloat16)
        taken = jnp.dot(place, ones, preferred_element_type=jnp.float32)[:, :1]
        for n in range(steps):
            columns = pl.ds(n * wide, wide)
            picked = jnp.dot(place, tokens_ref[:, columns], preferred_element_type=jnp.float32)
            if n == 0:
                picked = picked + jnp.where(lane == 0, EMPTY * (1.0 - taken), 0.0)
            spot = pl.ds(c * rows, rows)
            out[spot, columns] = picked.astype(out.dtype)
            copy = pltpu.make_async_copy(
                out.at[spot, columns], out_hbm.at[spot, columns], sems.at[c * steps + n]
            )
            copy.start()
            copies.append(copy)
    for copy in copies:
        copy.wait()


def place_rows(routes, tokens, experts, part):
    tok_rows, half = tokens.shape
    shape = (2 * experts * part, half)
    wide = 256
    return pl.pallas_call(
        functools.partial(route_kernel, experts, part, wide),
        out_shape=jax.ShapeDtypeStruct(shape, jnp.bfloat16),
        in_specs=[pl.BlockSpec(memory_space=pltpu.VMEM)] * 2,
        out_specs=pl.BlockSpec(memory_space=pltpu.HBM),
        scratch_shapes=[
            pltpu.VMEM(shape, jnp.bfloat16), pltpu.SemaphoreType.DMA((2 * (half // wide),))
        ],
        compiler_params=pltpu.CompilerParams(vmem_limit_bytes=VMEM_LIMIT),
    )(routes, tokens)


def expert_kernel(
    core_ref, x_hbm, gate_own, up_own, gate_other, up_other, down_own, down_other,
    out_hbm, hid_ref, count_ref, x, first, second, outs, x_sems, f_sems, s_sems, o_sems,
):
    core = core_ref[0]
    half = x.shape[2]
    ff_half = gate_own.shape[2]
    wide = 256

    def load_x(f):
        return pltpu.make_async_copy(x_hbm.at[f], x.at[f], x_sems.at[f])

    def load_first(i, src, f):
        return pltpu.make_async_copy(
            src.at[0, pl.ds(f * half, half)], first.at[i, f], f_sems.at[2 * i + f]
        )

    queue = []
    cut = 768
    for i, src in enumerate((gate_own, up_own, gate_other, up_other)):
        for f in range(2):
            if i == 0 and f == 0:
                for n, span in enumerate((pl.ds(0, cut), pl.ds(cut, half - cut))):
                    queue.append(
                        pltpu.make_async_copy(
                            x_hbm.at[0, :, span], x.at[0, :, span], x_sems.at[2 * n]
                        )
                    )
                    queue.append(
                        pltpu.make_async_copy(
                            src.at[0, span], first.at[0, 0, span], f_sems.at[8 * n]
                        )
                    )
                continue
            if i == 0:
                queue.append(load_x(f))
            queue.append(load_first(i, src, f))
    for i, src in enumerate((down_own, down_other)):
        queue.append(pltpu.make_async_copy(src.at[0], second.at[i], s_sems.at[i]))
    started = []

    def ahead(count):
        while len(started) < min(count, len(queue)):
            copy = queue[len(started)]
            copy.start()
            started.append(copy)

    done = []

    def ready(count):
        while len(done) < count:
            queue[len(done)].wait()
            done.append(None)
            ahead(len(done) + LOOKAHEAD)

    ahead(LOOKAHEAD)

    def product(i):
        if i == 0:
            ready(2)
            total = jnp.dot(x[0, :, :cut], first[0, 0, :cut], preferred_element_type=jnp.float32)
            ready(4)
            total = total + jnp.dot(x[0, :, cut:], first[0, 0, cut:], preferred_element_type=jnp.float32)
        else:
            ready(5 + 2 * i)
            total = jnp.dot(x[0], first[i, 0], preferred_element_type=jnp.float32)
        ready(6 + 2 * i)
        return total + jnp.dot(x[1], first[i, 1], preferred_element_type=jnp.float32)

    for side in range(2):
        gate = product(2 * side)
        if side == 0:
            valid = x[0, :, :128].astype(jnp.float32)[:, :1] < EMPTY / 2
            count_ref[...] = jnp.full(count_ref.shape, jnp.sum(valid.astype(jnp.float32)))
        upper = product(2 * side + 1)
        hidden = jnp.where(valid, gate / (1.0 + jnp.exp(-gate)) * upper, 0.0)
        base = (core if side == 0 else 1 - core) * ff_half
        hid_ref[:, pl.ds(pl.multiple_of(base, ff_half), ff_half)] = hidden.astype(hid_ref.dtype)
    copies = []
    for side in range(2):
        ready(13 + side)
        target = core if side == 0 else 1 - core
        for n in range(half // wide):
            columns = pl.ds(n * wide, wide)
            outs[side, :, columns] = jnp.dot(
                hid_ref[...], second[side, :, columns], preferred_element_type=jnp.float32
            ).astype(outs.dtype)
            copy = pltpu.make_async_copy(
                outs.at[side, :, columns], out_hbm.at[target, :, columns],
                o_sems.at[side * (half // wide) + n],
            )
            copy.start()
            copies.append(copy)
    for copy in copies:
        copy.wait()


def run_experts(core, x, gate_own, up_own, gate_other, up_other, down_own, down_other):
    _, rows, half = x.shape
    width = 2 * half
    ff_half = gate_own.shape[2]
    ff = 2 * ff_half
    whole = pl.BlockSpec(memory_space=pltpu.VMEM)
    far = pl.BlockSpec(memory_space=pltpu.HBM)
    return pl.pallas_call(
        expert_kernel,
        out_shape=(
            jax.ShapeDtypeStruct((2, rows, half), jnp.bfloat16),
            jax.ShapeDtypeStruct((rows, ff), jnp.bfloat16),
            jax.ShapeDtypeStruct((8, 128), jnp.float32),
        ),
        in_specs=[pl.BlockSpec(memory_space=pltpu.SMEM)] + [far] * 7,
        out_specs=(far, whole, whole),
        scratch_shapes=[
            pltpu.VMEM((2, rows, half), jnp.bfloat16),
            pltpu.VMEM((4, 2, half, ff_half), jnp.bfloat16),
            pltpu.VMEM((2, ff, half), jnp.bfloat16),
            pltpu.VMEM((2, rows, half), jnp.bfloat16),
            pltpu.SemaphoreType.DMA((3,)),
            pltpu.SemaphoreType.DMA((9,)),
            pltpu.SemaphoreType.DMA((2,)),
            pltpu.SemaphoreType.DMA((2 * (half // 256),)),
        ],
        compiler_params=pltpu.CompilerParams(vmem_limit_bytes=VMEM_LIMIT),
        cost_estimate=pl.CostEstimate(
            flops=2 * rows * width * ff * 3, bytes_accessed=6 * width * ff + 4 * rows * width,
            transcendentals=rows * ff,
        ),
    )(core, x, gate_own, up_own, gate_other, up_other, down_own, down_other)


def mix_kernel(mixes_ref, returned_hbm, out_ref, returned, sems):
    tok_rows = out_ref.shape[0]
    parts, rows, _ = returned.shape
    copies = []
    for n in range(parts):
        span = pl.ds(n * rows, rows)
        copies.append(pltpu.make_async_copy(returned_hbm.at[span], returned.at[n], sems.at[n]))
        copies[-1].start()
    total = None
    for n, copy in enumerate(copies):
        copy.wait()
        both = jnp.dot(
            mixes_ref[:, n * rows : (n + 1) * rows], returned[n], preferred_element_type=jnp.float32
        )
        total = both if total is None else total + both
    out_ref[...] = (total[:tok_rows] + total[tok_rows:]).astype(out_ref.dtype)


def mix_rows(mixes, returned):
    rows, half = returned.shape
    parts = 4
    return pl.pallas_call(
        mix_kernel,
        out_shape=jax.ShapeDtypeStruct((mixes.shape[0] // 2, half), jnp.bfloat16),
        in_specs=[pl.BlockSpec(memory_space=pltpu.VMEM), pl.BlockSpec(memory_space=pltpu.HBM)],
        out_specs=pl.BlockSpec(memory_space=pltpu.VMEM),
        scratch_shapes=[
            pltpu.VMEM((parts, rows // parts, half), jnp.bfloat16),
            pltpu.SemaphoreType.DMA((parts,)),
        ],
        compiler_params=pltpu.CompilerParams(vmem_limit_bytes=VMEM_LIMIT),
    )(mixes, returned)


def swap(array):
    return lax.ppermute(array, "token", [(0, 1), (1, 0)])


def mix_table(routes, mixing, experts, part):
    tok_rows = routes.shape[0]
    names = jnp.arange(experts, dtype=jnp.int32)
    match = routes[:, :, None] == names[None, None, :]
    chosen = jnp.any(match, axis=1)
    weight = jnp.sum(jnp.where(match, mixing[:, :, None], 0.0), axis=1)
    spots = jnp.arange(tok_rows, dtype=jnp.int32)
    before = (spots[:, None] > spots[None, :]).astype(jnp.bfloat16)
    rank = jnp.dot(before, chosen.astype(jnp.bfloat16), preferred_element_type=jnp.float32)
    key = jnp.where(chosen, rank.astype(jnp.int32), -1)
    slot = jnp.arange(2 * part, dtype=jnp.int32).reshape(2, 1, part)
    place = key[:, None, :, None] == slot[None]
    mixes = jnp.where(place, weight[:, None, :, None], 0.0).reshape(tok_rows, -1)
    high = lax.reduce_precision(mixes, 8, 7)
    return jnp.concatenate([high, mixes - high], axis=0).astype(jnp.bfloat16)


def shards(tokens, routes, mixing, gate_weight, up_weight, down_weight):
    tok_rows, half = tokens.shape
    experts = lax.axis_size("expert")
    capacity = 2 * tok_rows * routes.shape[1] // experts
    part = capacity // 2
    core = lax.axis_index("token")
    outgoing = place_rows(routes.T, tokens, experts, part).reshape(2 * experts, part, half)
    received = lax.all_to_all(outgoing, ("token", "expert"), 0, 0, tiled=True)
    x = received.reshape(2, experts * part, half)
    _, gate_sent, up_sent, down_sent = lax.optimization_barrier(
        (outgoing, gate_weight, up_weight, down_weight)
    )
    gate_other, up_other, down_other = swap(gate_sent), swap(up_sent), swap(down_sent)
    out, hidden, count = run_experts(
        core.reshape(1), x, gate_weight, up_weight, gate_other, up_other, down_weight, down_other
    )
    returned = lax.all_to_all(
        out.reshape(2 * experts, part, half), ("token", "expert"), 0, 0, tiled=True
    ).reshape(-1, half)
    hidden_other, count_other = swap(hidden), swap(count)
    ff_half = gate_weight.shape[2]

    def outer(array):
        own = lax.dynamic_slice_in_dim(array, core * ff_half, ff_half, 1)
        return lax.dot_general(
            own, array, (((0,), (0,)), ((), ())), preferred_element_type=jnp.float32
        )

    total = count[0, 0] + count_other[0, 0]
    hessian = (2.0 / total * (outer(hidden) + outer(hidden_other)))[None]
    mixed = mix_rows(mix_table(routes, mixing, experts, part), returned)
    return mixed, hessian


def solution(mesh):
    placed = (
        P("expert", "token"),
        P("expert", None),
        P("expert", None),
        P("expert", None, "token"),
        P("expert", None, "token"),
        P("expert", None, "token"),
    )
    return jax.shard_map(
        shards,
        mesh=mesh,
        in_specs=placed,
        out_specs=(P("expert", "token"), P("expert", "token", None)),
        check_vma=False,
    )
```

```python
import functools

import jax
import jax.numpy as jnp
from jax import lax
from jax.experimental import pallas as pl
from jax.experimental.pallas import tpu as pltpu
from jax.sharding import PartitionSpec as P

EMPTY = 64.0
LOOKAHEAD = 4
VMEM_LIMIT = 61 * 1024 * 1024


def route_kernel(experts, part, wide, routes_ref, tokens_ref, out_hbm, out, sems):
    tok_rows, half = tokens_ref.shape
    steps = half // wide
    names = lax.broadcasted_iota(jnp.int32, (experts, tok_rows), 0)
    chosen = names == routes_ref[0:1, :]
    for k in range(1, routes_ref.shape[0]):
        chosen = chosen | (names == routes_ref[k : k + 1, :])
    first = lax.broadcasted_iota(jnp.int32, (tok_rows, tok_rows), 0)
    second = lax.broadcasted_iota(jnp.int32, (tok_rows, tok_rows), 1)
    rank = jnp.dot(
        chosen.astype(jnp.bfloat16), (first < second).astype(jnp.bfloat16),
        preferred_element_type=jnp.float32,
    )
    key = jnp.where(chosen, rank, -1.0)
    ones = jnp.ones((tok_rows, 128), jnp.bfloat16)
    group = experts // 2
    rows = group * 2 * part
    lane = lax.broadcasted_iota(jnp.int32, (rows, wide), 1)
    slot = lax.broadcasted_iota(jnp.int32, (group, 2 * part, tok_rows), 1).astype(jnp.float32)
    copies = []
    for c in range(2):
        place = jnp.where(key[c * group : (c + 1) * group, None, :] == slot, 1.0, 0.0)
        place = place.reshape(rows, tok_rows).astype(jnp.bfloat16)
        taken = jnp.dot(place, ones, preferred_element_type=jnp.float32)[:, :1]
        for n in range(steps):
            columns = pl.ds(n * wide, wide)
            picked = jnp.dot(place, tokens_ref[:, columns], preferred_element_type=jnp.float32)
            if n == 0:
                picked = picked + jnp.where(lane == 0, EMPTY * (1.0 - taken), 0.0)
            spot = pl.ds(c * rows, rows)
            out[spot, columns] = picked.astype(out.dtype)
            copy = pltpu.make_async_copy(
                out.at[spot, columns], out_hbm.at[spot, columns], sems.at[c * steps + n]
            )
            copy.start()
            copies.append(copy)
    for copy in copies:
        copy.wait()


def place_rows(routes, tokens, experts, part):
    tok_rows, half = tokens.shape
    shape = (2 * experts * part, half)
    wide = 256
    return pl.pallas_call(
        functools.partial(route_kernel, experts, part, wide),
        out_shape=jax.ShapeDtypeStruct(shape, jnp.bfloat16),
        in_specs=[pl.BlockSpec(memory_space=pltpu.VMEM)] * 2,
        out_specs=pl.BlockSpec(memory_space=pltpu.HBM),
        scratch_shapes=[
            pltpu.VMEM(shape, jnp.bfloat16), pltpu.SemaphoreType.DMA((2 * (half // wide),))
        ],
        compiler_params=pltpu.CompilerParams(vmem_limit_bytes=VMEM_LIMIT),
    )(routes, tokens)


def expert_kernel(
    core_ref, x_hbm, gate_own, up_own, gate_other, up_other, down_own, down_other,
    out_hbm, hid_ref, count_ref, x, first, second, outs, x_sems, f_sems, s_sems, o_sems,
):
    core = core_ref[0]
    _, groups, part, half = x.shape
    rows = groups * part
    ff_half = gate_own.shape[2]
    wide = 256

    def load_x(f):
        return pltpu.make_async_copy(x_hbm.at[:, f], x.at[f], x_sems.at[f])

    def load_first(i, src, f):
        return pltpu.make_async_copy(
            src.at[0, pl.ds(f * half, half)], first.at[i, f], f_sems.at[2 * i + f]
        )

    queue = []
    cut = 768
    for i, src in enumerate((gate_own, up_own, gate_other, up_other)):
        for f in range(2):
            if i == 0 and f == 0:
                for n, span in enumerate((pl.ds(0, cut), pl.ds(cut, half - cut))):
                    queue.append(
                        pltpu.make_async_copy(
                            x_hbm.at[:, 0, :, span], x.at[0, :, :, span], x_sems.at[2 * n]
                        )
                    )
                    queue.append(
                        pltpu.make_async_copy(
                            src.at[0, span], first.at[0, 0, span], f_sems.at[8 * n]
                        )
                    )
                continue
            if i == 0:
                queue.append(load_x(f))
            queue.append(load_first(i, src, f))
    for i, src in enumerate((down_own, down_other)):
        queue.append(pltpu.make_async_copy(src.at[0], second.at[i], s_sems.at[i]))
    started = []

    def ahead(count):
        while len(started) < min(count, len(queue)):
            copy = queue[len(started)]
            copy.start()
            started.append(copy)

    done = []

    def ready(count):
        while len(done) < count:
            queue[len(done)].wait()
            done.append(None)
            ahead(len(done) + LOOKAHEAD)

    ahead(LOOKAHEAD)

    def product(i):
        if i == 0:
            ready(2)
            total = jnp.dot(x[0, :, :, :cut].reshape(rows, cut), first[0, 0, :cut], preferred_element_type=jnp.float32)
            ready(4)
            total = total + jnp.dot(x[0, :, :, cut:].reshape(rows, half - cut), first[0, 0, cut:], preferred_element_type=jnp.float32)
        else:
            ready(5 + 2 * i)
            total = jnp.dot(x[0].reshape(rows, half), first[i, 0], preferred_element_type=jnp.float32)
        ready(6 + 2 * i)
        return total + jnp.dot(x[1].reshape(rows, half), first[i, 1], preferred_element_type=jnp.float32)

    for side in range(2):
        gate = product(2 * side)
        if side == 0:
            valid = x[0, :, :, :128].astype(jnp.float32).reshape(rows, 128)[:, :1] < EMPTY / 2
            count_ref[...] = jnp.full(count_ref.shape, jnp.sum(valid.astype(jnp.float32)))
        upper = product(2 * side + 1)
        hidden = jnp.where(valid, gate / (1.0 + jnp.exp(-gate)) * upper, 0.0)
        base = (core if side == 0 else 1 - core) * ff_half
        hid_ref[:, pl.ds(pl.multiple_of(base, ff_half), ff_half)] = hidden.astype(hid_ref.dtype)
    copies = []
    for side in range(2):
        ready(13 + side)
        target = core if side == 0 else 1 - core
        for n in range(half // wide):
            columns = pl.ds(n * wide, wide)
            result = jnp.dot(
                hid_ref[...], second[side, :, columns], preferred_element_type=jnp.float32
            )
            outs[side, :, :, columns] = result.reshape(groups, part, wide).astype(outs.dtype)
            copy = pltpu.make_async_copy(
                outs.at[side, :, :, columns], out_hbm.at[:, target, :, columns],
                o_sems.at[side * (half // wide) + n],
            )
            copy.start()
            copies.append(copy)
    for copy in copies:
        copy.wait()


def run_experts(core, x, gate_own, up_own, gate_other, up_other, down_own, down_other):
    groups, _, part, half = x.shape
    rows = groups * part
    width = 2 * half
    ff_half = gate_own.shape[2]
    ff = 2 * ff_half
    whole = pl.BlockSpec(memory_space=pltpu.VMEM)
    far = pl.BlockSpec(memory_space=pltpu.HBM)
    return pl.pallas_call(
        expert_kernel,
        out_shape=(
            jax.ShapeDtypeStruct((groups, 2, part, half), jnp.bfloat16),
            jax.ShapeDtypeStruct((rows, ff), jnp.bfloat16),
            jax.ShapeDtypeStruct((8, 128), jnp.float32),
        ),
        in_specs=[pl.BlockSpec(memory_space=pltpu.SMEM)] + [far] * 7,
        out_specs=(far, whole, whole),
        scratch_shapes=[
            pltpu.VMEM((2, groups, part, half), jnp.bfloat16),
            pltpu.VMEM((4, 2, half, ff_half), jnp.bfloat16),
            pltpu.VMEM((2, ff, half), jnp.bfloat16),
            pltpu.VMEM((2, groups, part, half), jnp.bfloat16),
            pltpu.SemaphoreType.DMA((3,)),
            pltpu.SemaphoreType.DMA((9,)),
            pltpu.SemaphoreType.DMA((2,)),
            pltpu.SemaphoreType.DMA((2 * (half // 256),)),
        ],
        compiler_params=pltpu.CompilerParams(vmem_limit_bytes=VMEM_LIMIT),
        cost_estimate=pl.CostEstimate(
            flops=2 * rows * width * ff * 3, bytes_accessed=6 * width * ff + 4 * rows * width,
            transcendentals=rows * ff,
        ),
    )(core, x, gate_own, up_own, gate_other, up_other, down_own, down_other)


def mix_kernel(mixes_ref, returned_hbm, out_ref, returned, sems):
    tok_rows = out_ref.shape[0]
    parts, rows, _ = returned.shape
    copies = []
    for n in range(parts):
        span = pl.ds(n * rows, rows)
        copies.append(pltpu.make_async_copy(returned_hbm.at[span], returned.at[n], sems.at[n]))
        copies[-1].start()
    total = None
    for n, copy in enumerate(copies):
        copy.wait()
        both = jnp.dot(
            mixes_ref[:, n * rows : (n + 1) * rows], returned[n], preferred_element_type=jnp.float32
        )
        total = both if total is None else total + both
    out_ref[...] = (total[:tok_rows] + total[tok_rows:]).astype(out_ref.dtype)


def mix_rows(mixes, returned):
    rows, half = returned.shape
    parts = 4
    return pl.pallas_call(
        mix_kernel,
        out_shape=jax.ShapeDtypeStruct((mixes.shape[0] // 2, half), jnp.bfloat16),
        in_specs=[pl.BlockSpec(memory_space=pltpu.VMEM), pl.BlockSpec(memory_space=pltpu.HBM)],
        out_specs=pl.BlockSpec(memory_space=pltpu.VMEM),
        scratch_shapes=[
            pltpu.VMEM((parts, rows // parts, half), jnp.bfloat16),
            pltpu.SemaphoreType.DMA((parts,)),
        ],
        compiler_params=pltpu.CompilerParams(vmem_limit_bytes=VMEM_LIMIT),
    )(mixes, returned)


def swap(array):
    return lax.ppermute(array, "token", [(0, 1), (1, 0)])


def mix_table(routes, mixing, experts, part):
    tok_rows = routes.shape[0]
    names = jnp.arange(experts, dtype=jnp.int32)
    match = routes[:, :, None] == names[None, None, :]
    chosen = jnp.any(match, axis=1)
    weight = jnp.sum(jnp.where(match, mixing[:, :, None], 0.0), axis=1)
    spots = jnp.arange(tok_rows, dtype=jnp.int32)
    before = (spots[:, None] > spots[None, :]).astype(jnp.bfloat16)
    rank = jnp.dot(before, chosen.astype(jnp.bfloat16), preferred_element_type=jnp.float32)
    key = jnp.where(chosen, rank.astype(jnp.int32), -1)
    slot = jnp.arange(2 * part, dtype=jnp.int32)
    place = key[:, :, None] == slot
    mixes = jnp.where(place, weight[:, :, None], 0.0).reshape(tok_rows, -1)
    high = lax.reduce_precision(mixes, 8, 7)
    return jnp.concatenate([high, mixes - high], axis=0).astype(jnp.bfloat16)


def shards(tokens, routes, mixing, gate_weight, up_weight, down_weight):
    tok_rows, half = tokens.shape
    experts = lax.axis_size("expert")
    capacity = 2 * tok_rows * routes.shape[1] // experts
    part = capacity // 2
    core = lax.axis_index("token")
    outgoing = place_rows(routes.T, tokens, experts, part).reshape(2 * experts, part, half)
    received = lax.all_to_all(outgoing, ("expert", "token"), 0, 0, tiled=True)
    x = received.reshape(experts, 2, part, half)
    _, gate_sent, up_sent, down_sent = lax.optimization_barrier(
        (outgoing, gate_weight, up_weight, down_weight)
    )
    gate_other, up_other, down_other = swap(gate_sent), swap(up_sent), swap(down_sent)
    out, hidden, count = run_experts(
        core.reshape(1), x, gate_weight, up_weight, gate_other, up_other, down_weight, down_other
    )
    returned = lax.all_to_all(
        out.reshape(2 * experts, part, half), ("expert", "token"), 0, 0, tiled=True
    ).reshape(-1, half)
    hidden_other, count_other = swap(hidden), swap(count)
    ff_half = gate_weight.shape[2]

    def outer(array):
        own = lax.dynamic_slice_in_dim(array, core * ff_half, ff_half, 1)
        return lax.dot_general(
            own, array, (((0,), (0,)), ((), ())), preferred_element_type=jnp.float32
        )

    total = count[0, 0] + count_other[0, 0]
    hessian = (2.0 / total * (outer(hidden) + outer(hidden_other)))[None]
    mixed = mix_rows(mix_table(routes, mixing, experts, part), returned)
    return mixed, hessian


def solution(mesh):
    placed = (
        P("expert", "token"),
        P("expert", None),
        P("expert", None),
        P("expert", None, "token"),
        P("expert", None, "token"),
        P("expert", None, "token"),
    )
    return jax.shard_map(
        shards,
        mesh=mesh,
        in_specs=placed,
        out_specs=(P("expert", "token"), P("expert", "token", None)),
        check_vma=False,
    )
```

```python
import functools

import jax
import jax.numpy as jnp
from jax import lax
from jax.experimental import pallas as pl
from jax.experimental.pallas import tpu as pltpu
from jax.sharding import PartitionSpec as P

EMPTY = 64.0
LOOKAHEAD = 4
VMEM_LIMIT = 61 * 1024 * 1024


def route_kernel(experts, part, wide, routes_ref, tokens_ref, out_hbm, out, sems):
    tok_rows, half = tokens_ref.shape
    steps = half // wide
    names = lax.broadcasted_iota(jnp.int32, (experts, tok_rows), 0)
    chosen = names == routes_ref[0:1, :]
    for k in range(1, routes_ref.shape[0]):
        chosen = chosen | (names == routes_ref[k : k + 1, :])
    first = lax.broadcasted_iota(jnp.int32, (tok_rows, tok_rows), 0)
    second = lax.broadcasted_iota(jnp.int32, (tok_rows, tok_rows), 1)
    rank = jnp.dot(
        chosen.astype(jnp.bfloat16), (first < second).astype(jnp.bfloat16),
        preferred_element_type=jnp.float32,
    )
    key = jnp.where(chosen, rank, -1.0)
    ones = jnp.ones((tok_rows, 128), jnp.bfloat16)
    group = experts // 2
    rows = group * 2 * part
    lane = lax.broadcasted_iota(jnp.int32, (rows, wide), 1)
    slot = lax.broadcasted_iota(jnp.int32, (group, 2 * part, tok_rows), 1).astype(jnp.float32)
    copies = []
    for c in range(2):
        place = jnp.where(key[c * group : (c + 1) * group, None, :] == slot, 1.0, 0.0)
        place = place.reshape(rows, tok_rows).astype(jnp.bfloat16)
        taken = jnp.dot(place, ones, preferred_element_type=jnp.float32)[:, :1]
        for n in range(steps):
            columns = pl.ds(n * wide, wide)
            picked = jnp.dot(place, tokens_ref[:, columns], preferred_element_type=jnp.float32)
            if n == 0:
                picked = picked + jnp.where(lane == 0, EMPTY * (1.0 - taken), 0.0)
            spot = pl.ds(c * rows, rows)
            out[spot, columns] = picked.astype(out.dtype)
            copy = pltpu.make_async_copy(
                out.at[spot, columns], out_hbm.at[spot, columns], sems.at[c * steps + n]
            )
            copy.start()
            copies.append(copy)
    for copy in copies:
        copy.wait()


def place_rows(routes, tokens, experts, part):
    tok_rows, half = tokens.shape
    shape = (2 * experts * part, half)
    wide = 256
    return pl.pallas_call(
        functools.partial(route_kernel, experts, part, wide),
        out_shape=jax.ShapeDtypeStruct(shape, jnp.bfloat16),
        in_specs=[pl.BlockSpec(memory_space=pltpu.VMEM)] * 2,
        out_specs=pl.BlockSpec(memory_space=pltpu.HBM),
        scratch_shapes=[
            pltpu.VMEM(shape, jnp.bfloat16), pltpu.SemaphoreType.DMA((2 * (half // wide),))
        ],
        compiler_params=pltpu.CompilerParams(vmem_limit_bytes=VMEM_LIMIT),
    )(routes, tokens)


def expert_kernel(
    core_ref, x_hbm, gate_own, up_own, gate_other, up_other, down_own, down_other,
    out_hbm, hid_ref, count_ref, x, first, second, outs, x_sems, f_sems, s_sems, o_sems,
):
    core = core_ref[0]
    _, groups, part, half = x.shape
    rows = groups * part
    ff_half = gate_own.shape[2]
    wide = 256

    def load_x(f):
        return pltpu.make_async_copy(x_hbm.at[:, f], x.at[f], x_sems.at[f])

    def load_first(i, src, f):
        return pltpu.make_async_copy(
            src.at[0, pl.ds(f * half, half)], first.at[i, f], f_sems.at[2 * i + f]
        )

    queue = []
    cut = 768
    for i, src in enumerate((gate_own, up_own, gate_other, up_other)):
        for f in range(2):
            if i == 0 and f == 0:
                for n, span in enumerate((pl.ds(0, cut), pl.ds(cut, half - cut))):
                    queue.append(
                        pltpu.make_async_copy(
                            x_hbm.at[:, 0, :, span], x.at[0, :, :, span], x_sems.at[2 * n]
                        )
                    )
                    queue.append(
                        pltpu.make_async_copy(
                            src.at[0, span], first.at[0, 0, span], f_sems.at[8 * n]
                        )
                    )
                continue
            if i == 0:
                queue.append(load_x(f))
            queue.append(load_first(i, src, f))
    for i, src in enumerate((down_own, down_other)):
        queue.append(pltpu.make_async_copy(src.at[0], second.at[i], s_sems.at[i]))
    started = []

    def ahead(count):
        while len(started) < min(count, len(queue)):
            copy = queue[len(started)]
            copy.start()
            started.append(copy)

    done = []

    def ready(count):
        while len(done) < count:
            queue[len(done)].wait()
            done.append(None)
            ahead(len(done) + LOOKAHEAD)

    ahead(LOOKAHEAD)

    def features(f):
        return x[f].reshape(rows, half)

    def product(i):
        return jnp.dot(
            features(0), first[i, 0], preferred_element_type=jnp.float32
        ) + jnp.dot(features(1), first[i, 1], preferred_element_type=jnp.float32)

    def keep(side, gate, upper):
        hidden = jnp.where(valid, gate / (1.0 + jnp.exp(-gate)) * upper, 0.0)
        base = (core if side == 0 else 1 - core) * ff_half
        hid_ref[:, pl.ds(pl.multiple_of(base, ff_half), ff_half)] = hidden.astype(hid_ref.dtype)

    ready(2)
    gate = jnp.dot(
        x[0, :, :, :cut].reshape(rows, cut), first[0, 0, :cut], preferred_element_type=jnp.float32
    )
    ready(4)
    gate = gate + jnp.dot(
        x[0, :, :, cut:].reshape(rows, half - cut), first[0, 0, cut:],
        preferred_element_type=jnp.float32,
    )
    ready(6)
    gate = gate + jnp.dot(features(1), first[0, 1], preferred_element_type=jnp.float32)
    valid = x[0, :, :, :128].astype(jnp.float32).reshape(rows, 128)[:, :1] < EMPTY / 2
    count_ref[...] = jnp.full(count_ref.shape, jnp.sum(valid.astype(jnp.float32)))
    ready(8)
    upper = product(1)
    ready(10)
    keep(0, gate, upper)
    gate = product(2)
    ready(12)
    keep(1, gate, product(3))
    copies = []
    for side in range(2):
        ready(13 + side)
        target = core if side == 0 else 1 - core
        for n in range(half // wide):
            columns = pl.ds(n * wide, wide)
            result = jnp.dot(
                hid_ref[...], second[side, :, columns], preferred_element_type=jnp.float32
            )
            outs[side, :, :, columns] = result.reshape(groups, part, wide).astype(outs.dtype)
            copy = pltpu.make_async_copy(
                outs.at[side, :, :, columns], out_hbm.at[:, target, :, columns],
                o_sems.at[side * (half // wide) + n],
            )
            copy.start()
            copies.append(copy)
    for copy in copies:
        copy.wait()


def run_experts(core, x, gate_own, up_own, gate_other, up_other, down_own, down_other):
    groups, _, part, half = x.shape
    rows = groups * part
    width = 2 * half
    ff_half = gate_own.shape[2]
    ff = 2 * ff_half
    whole = pl.BlockSpec(memory_space=pltpu.VMEM)
    far = pl.BlockSpec(memory_space=pltpu.HBM)
    return pl.pallas_call(
        expert_kernel,
        out_shape=(
            jax.ShapeDtypeStruct((groups, 2, part, half), jnp.bfloat16),
            jax.ShapeDtypeStruct((rows, ff), jnp.bfloat16),
            jax.ShapeDtypeStruct((8, 128), jnp.float32),
        ),
        in_specs=[pl.BlockSpec(memory_space=pltpu.SMEM)] + [far] * 7,
        out_specs=(far, whole, whole),
        scratch_shapes=[
            pltpu.VMEM((2, groups, part, half), jnp.bfloat16),
            pltpu.VMEM((4, 2, half, ff_half), jnp.bfloat16),
            pltpu.VMEM((2, ff, half), jnp.bfloat16),
            pltpu.VMEM((2, groups, part, half), jnp.bfloat16),
            pltpu.SemaphoreType.DMA((3,)),
            pltpu.SemaphoreType.DMA((9,)),
            pltpu.SemaphoreType.DMA((2,)),
            pltpu.SemaphoreType.DMA((2 * (half // 256),)),
        ],
        compiler_params=pltpu.CompilerParams(vmem_limit_bytes=VMEM_LIMIT),
        cost_estimate=pl.CostEstimate(
            flops=2 * rows * width * ff * 3, bytes_accessed=6 * width * ff + 4 * rows * width,
            transcendentals=rows * ff,
        ),
    )(core, x, gate_own, up_own, gate_other, up_other, down_own, down_other)


def swap(array):
    return lax.ppermute(array, "token", [(0, 1), (1, 0)])


def mix_table(routes, mixing, experts, part):
    tok_rows = routes.shape[0]
    names = jnp.arange(experts, dtype=jnp.int32)
    match = routes[:, :, None] == names[None, None, :]
    chosen = jnp.any(match, axis=1)
    weight = jnp.sum(jnp.where(match, mixing[:, :, None], 0.0), axis=1)
    spots = jnp.arange(tok_rows, dtype=jnp.int32)
    before = (spots[:, None] > spots[None, :]).astype(jnp.bfloat16)
    rank = jnp.dot(before, chosen.astype(jnp.bfloat16), preferred_element_type=jnp.float32)
    key = jnp.where(chosen, rank.astype(jnp.int32), -1)
    slot = jnp.arange(2 * part, dtype=jnp.int32)
    place = key[:, :, None] == slot
    mixes = jnp.where(place, weight[:, :, None], 0.0).reshape(tok_rows, -1)
    high = lax.reduce_precision(mixes, 8, 7)
    return high.astype(jnp.bfloat16), (mixes - high).astype(jnp.bfloat16)


def shards(tokens, routes, mixing, gate_weight, up_weight, down_weight):
    tok_rows, half = tokens.shape
    experts = lax.axis_size("expert")
    capacity = 2 * tok_rows * routes.shape[1] // experts
    part = capacity // 2
    core = lax.axis_index("token")
    outgoing = place_rows(routes.T, tokens, experts, part).reshape(2 * experts, part, half)
    received = lax.all_to_all(outgoing, ("expert", "token"), 0, 0, tiled=True)
    x = received.reshape(experts, 2, part, half)
    _, gate_sent, up_sent, down_sent = lax.optimization_barrier(
        (outgoing, gate_weight, up_weight, down_weight)
    )
    gate_other, up_other, down_other = swap(gate_sent), swap(up_sent), swap(down_sent)
    out, hidden, count = run_experts(
        core.reshape(1), x, gate_weight, up_weight, gate_other, up_other, down_weight, down_other
    )
    returned = lax.all_to_all(
        out.reshape(2 * experts, part, half), ("expert", "token"), 0, 0, tiled=True
    ).reshape(-1, half)
    hidden_other, count_other = swap(hidden), swap(count)
    ff_half = gate_weight.shape[2]

    def outer(array):
        own = lax.dynamic_slice_in_dim(array, core * ff_half, ff_half, 1)
        return lax.dot_general(
            own, array, (((0,), (0,)), ((), ())), preferred_element_type=jnp.float32
        )

    total = count[0, 0] + count_other[0, 0]
    hessian = (2.0 / total * (outer(hidden) + outer(hidden_other)))[None]
    high, low = mix_table(routes, mixing, experts, part)
    mixed = jnp.dot(jnp.concatenate([high, low]), returned, preferred_element_type=jnp.float32)
    mixed = (mixed[:tok_rows] + mixed[tok_rows:]).astype(jnp.bfloat16)
    return mixed, hessian


def solution(mesh):
    placed = (
        P("expert", "token"),
        P("expert", None),
        P("expert", None),
        P("expert", None, "token"),
        P("expert", None, "token"),
        P("expert", None, "token"),
    )
    return jax.shard_map(
        shards,
        mesh=mesh,
        in_specs=placed,
        out_specs=(P("expert", "token"), P("expert", "token", None)),
        check_vma=False,
    )
```

```python
import functools

import jax
import jax.numpy as jnp
from jax import lax
from jax.experimental import pallas as pl
from jax.experimental.pallas import tpu as pltpu
from jax.sharding import PartitionSpec as P

EMPTY = 64.0
LOOKAHEAD = 4
VMEM_LIMIT = 61 * 1024 * 1024


def route_kernel(experts, part, wide, routes_hbm, tokens_hbm, out_hbm, routes_ref, tokens_ref, out, sems):
    tok_rows, half = tokens_ref.shape
    steps = half // wide
    load_routes = pltpu.make_async_copy(routes_hbm, routes_ref, sems.at[2 * steps])
    load_tokens = pltpu.make_async_copy(tokens_hbm, tokens_ref, sems.at[2 * steps + 1])
    load_routes.start()
    load_tokens.start()
    load_routes.wait()
    names = lax.broadcasted_iota(jnp.int32, (experts, tok_rows), 0)
    chosen = names == routes_ref[0:1, :]
    for k in range(1, routes_ref.shape[0]):
        chosen = chosen | (names == routes_ref[k : k + 1, :])
    first = lax.broadcasted_iota(jnp.int32, (tok_rows, tok_rows), 0)
    second = lax.broadcasted_iota(jnp.int32, (tok_rows, tok_rows), 1)
    rank = jnp.dot(
        chosen.astype(jnp.bfloat16), (first < second).astype(jnp.bfloat16),
        preferred_element_type=jnp.float32,
    )
    key = jnp.where(chosen, rank, -1.0)
    ones = jnp.ones((tok_rows, 128), jnp.bfloat16)
    group = experts // 2
    rows = group * 2 * part
    lane = lax.broadcasted_iota(jnp.int32, (rows, wide), 1)
    slot = lax.broadcasted_iota(jnp.int32, (group, 2 * part, tok_rows), 1).astype(jnp.float32)
    load_tokens.wait()
    copies = []
    for c in range(2):
        place = jnp.where(key[c * group : (c + 1) * group, None, :] == slot, 1.0, 0.0)
        place = place.reshape(rows, tok_rows).astype(jnp.bfloat16)
        taken = jnp.dot(place, ones, preferred_element_type=jnp.float32)[:, :1]
        for n in range(steps):
            columns = pl.ds(n * wide, wide)
            picked = jnp.dot(place, tokens_ref[:, columns], preferred_element_type=jnp.float32)
            if n == 0:
                picked = picked + jnp.where(lane == 0, EMPTY * (1.0 - taken), 0.0)
            spot = pl.ds(c * rows, rows)
            out[spot, columns] = picked.astype(out.dtype)
            copy = pltpu.make_async_copy(
                out.at[spot, columns], out_hbm.at[spot, columns], sems.at[c * steps + n]
            )
            copy.start()
            copies.append(copy)
    for copy in copies:
        copy.wait()


def place_rows(routes, tokens, experts, part):
    tok_rows, half = tokens.shape
    shape = (2 * experts * part, half)
    wide = 256
    return pl.pallas_call(
        functools.partial(route_kernel, experts, part, wide),
        out_shape=jax.ShapeDtypeStruct(shape, jnp.bfloat16),
        in_specs=[pl.BlockSpec(memory_space=pltpu.HBM)] * 2,
        out_specs=pl.BlockSpec(memory_space=pltpu.HBM),
        scratch_shapes=[
            pltpu.VMEM(routes.shape, routes.dtype),
            pltpu.VMEM(tokens.shape, tokens.dtype),
            pltpu.VMEM(shape, jnp.bfloat16),
            pltpu.SemaphoreType.DMA((2 * (half // wide) + 2,)),
        ],
        compiler_params=pltpu.CompilerParams(vmem_limit_bytes=VMEM_LIMIT),
    )(routes, tokens)


def expert_kernel(
    core_ref, x_hbm, gate_own, up_own, gate_other, up_other, down_own, down_other,
    out_hbm, hid_hbm, count_hbm, x, first, second, outs, hid_ref, count_ref,
    x_sems, f_sems, s_sems, o_sems, e_sems,
):
    core = core_ref[0]
    _, groups, part, half = x.shape
    rows = groups * part
    ff_half = gate_own.shape[2]
    wide = 256

    def load_x(f):
        return pltpu.make_async_copy(x_hbm.at[:, f], x.at[f], x_sems.at[f])

    def load_first(i, src, f):
        return pltpu.make_async_copy(
            src.at[0, pl.ds(f * half, half)], first.at[i, f], f_sems.at[2 * i + f]
        )

    queue = []
    cut = 768
    for i, src in enumerate((gate_own, up_own, gate_other, up_other)):
        for f in range(2):
            if i == 0 and f == 0:
                for n, span in enumerate((pl.ds(0, cut), pl.ds(cut, half - cut))):
                    queue.append(
                        pltpu.make_async_copy(
                            x_hbm.at[:, 0, :, span], x.at[0, :, :, span], x_sems.at[2 * n]
                        )
                    )
                    queue.append(
                        pltpu.make_async_copy(
                            src.at[0, span], first.at[0, 0, span], f_sems.at[8 * n]
                        )
                    )
                continue
            if i == 0:
                queue.append(load_x(f))
            queue.append(load_first(i, src, f))
    for i, src in enumerate((down_own, down_other)):
        queue.append(pltpu.make_async_copy(src.at[0], second.at[i], s_sems.at[i]))
    started = []

    def ahead(count):
        while len(started) < min(count, len(queue)):
            copy = queue[len(started)]
            copy.start()
            started.append(copy)

    done = []

    def ready(count):
        while len(done) < count:
            queue[len(done)].wait()
            done.append(None)
            ahead(len(done) + LOOKAHEAD)

    ahead(LOOKAHEAD)

    def features(f):
        return x[f].reshape(rows, half)

    def product(i):
        return jnp.dot(
            features(0), first[i, 0], preferred_element_type=jnp.float32
        ) + jnp.dot(features(1), first[i, 1], preferred_element_type=jnp.float32)

    def keep(side, gate, upper):
        hidden = jnp.where(valid, gate / (1.0 + jnp.exp(-gate)) * upper, 0.0)
        base = (core if side == 0 else 1 - core) * ff_half
        hid_ref[:, pl.ds(pl.multiple_of(base, ff_half), ff_half)] = hidden.astype(hid_ref.dtype)

    ready(2)
    gate = jnp.dot(
        x[0, :, :, :cut].reshape(rows, cut), first[0, 0, :cut], preferred_element_type=jnp.float32
    )
    ready(4)
    gate = gate + jnp.dot(
        x[0, :, :, cut:].reshape(rows, half - cut), first[0, 0, cut:],
        preferred_element_type=jnp.float32,
    )
    ready(6)
    gate = gate + jnp.dot(features(1), first[0, 1], preferred_element_type=jnp.float32)
    valid = x[0, :, :, :128].astype(jnp.float32).reshape(rows, 128)[:, :1] < EMPTY / 2
    count_ref[...] = jnp.full(count_ref.shape, jnp.sum(valid.astype(jnp.float32)))
    copies = [pltpu.make_async_copy(count_ref, count_hbm, e_sems.at[0])]
    copies[0].start()
    ready(8)
    upper = product(1)
    ready(10)
    keep(0, gate, upper)
    gate = product(2)
    ready(12)
    keep(1, gate, product(3))
    copies.append(pltpu.make_async_copy(hid_ref, hid_hbm, e_sems.at[1]))
    copies[1].start()
    for side in range(2):
        ready(13 + side)
        target = core if side == 0 else 1 - core
        for n in range(half // wide):
            columns = pl.ds(n * wide, wide)
            result = jnp.dot(
                hid_ref[...], second[side, :, columns], preferred_element_type=jnp.float32
            )
            outs[side, :, :, columns] = result.reshape(groups, part, wide).astype(outs.dtype)
            copy = pltpu.make_async_copy(
                outs.at[side, :, :, columns], out_hbm.at[:, target, :, columns],
                o_sems.at[side * (half // wide) + n],
            )
            copy.start()
            copies.append(copy)
    for copy in copies:
        copy.wait()


def run_experts(core, x, gate_own, up_own, gate_other, up_other, down_own, down_other):
    groups, _, part, half = x.shape
    rows = groups * part
    width = 2 * half
    ff_half = gate_own.shape[2]
    ff = 2 * ff_half
    far = pl.BlockSpec(memory_space=pltpu.HBM)
    return pl.pallas_call(
        expert_kernel,
        out_shape=(
            jax.ShapeDtypeStruct((groups, 2, part, half), jnp.bfloat16),
            jax.ShapeDtypeStruct((rows, ff), jnp.bfloat16),
            jax.ShapeDtypeStruct((8, 128), jnp.float32),
        ),
        in_specs=[pl.BlockSpec(memory_space=pltpu.SMEM)] + [far] * 7,
        out_specs=(far, far, far),
        scratch_shapes=[
            pltpu.VMEM((2, groups, part, half), jnp.bfloat16),
            pltpu.VMEM((4, 2, half, ff_half), jnp.bfloat16),
            pltpu.VMEM((2, ff, half), jnp.bfloat16),
            pltpu.VMEM((2, groups, part, half), jnp.bfloat16),
            pltpu.VMEM((rows, ff), jnp.bfloat16),
            pltpu.VMEM((8, 128), jnp.float32),
            pltpu.SemaphoreType.DMA((3,)),
            pltpu.SemaphoreType.DMA((9,)),
            pltpu.SemaphoreType.DMA((2,)),
            pltpu.SemaphoreType.DMA((2 * (half // 256),)),
            pltpu.SemaphoreType.DMA((2,)),
        ],
        compiler_params=pltpu.CompilerParams(vmem_limit_bytes=VMEM_LIMIT),
        cost_estimate=pl.CostEstimate(
            flops=2 * rows * width * ff * 3, bytes_accessed=6 * width * ff + 4 * rows * width,
            transcendentals=rows * ff,
        ),
    )(core, x, gate_own, up_own, gate_other, up_other, down_own, down_other)


def swap(array):
    return lax.ppermute(array, "token", [(0, 1), (1, 0)])


def mix_table(routes, mixing, experts, part):
    tok_rows = routes.shape[0]
    names = jnp.arange(experts, dtype=jnp.int32)
    match = routes[:, :, None] == names[None, None, :]
    chosen = jnp.any(match, axis=1)
    weight = jnp.sum(jnp.where(match, mixing[:, :, None], 0.0), axis=1)
    spots = jnp.arange(tok_rows, dtype=jnp.int32)
    before = (spots[:, None] > spots[None, :]).astype(jnp.bfloat16)
    rank = jnp.dot(before, chosen.astype(jnp.bfloat16), preferred_element_type=jnp.float32)
    key = jnp.where(chosen, rank.astype(jnp.int32), -1)
    slot = jnp.arange(2 * part, dtype=jnp.int32)
    place = key[:, :, None] == slot
    mixes = jnp.where(place, weight[:, :, None], 0.0).reshape(tok_rows, -1)
    high = lax.reduce_precision(mixes, 8, 7)
    return high.astype(jnp.bfloat16), (mixes - high).astype(jnp.bfloat16)


def shards(tokens, routes, mixing, gate_weight, up_weight, down_weight):
    tok_rows, half = tokens.shape
    experts = lax.axis_size("expert")
    capacity = 2 * tok_rows * routes.shape[1] // experts
    part = capacity // 2
    core = lax.axis_index("token")
    outgoing = place_rows(routes.T, tokens, experts, part).reshape(2 * experts, part, half)
    received = lax.all_to_all(outgoing, ("expert", "token"), 0, 0, tiled=True)
    x = received.reshape(experts, 2, part, half)
    _, gate_sent, up_sent, down_sent = lax.optimization_barrier(
        (outgoing, gate_weight, up_weight, down_weight)
    )
    gate_other, up_other, down_other = swap(gate_sent), swap(up_sent), swap(down_sent)
    out, hidden, count = run_experts(
        core.reshape(1), x, gate_weight, up_weight, gate_other, up_other, down_weight, down_other
    )
    returned = lax.all_to_all(
        out.reshape(2 * experts, part, half), ("expert", "token"), 0, 0, tiled=True
    ).reshape(-1, half)
    hidden_other, count_other = swap(hidden), swap(count)
    ff_half = gate_weight.shape[2]

    def outer(array):
        own = lax.dynamic_slice_in_dim(array, core * ff_half, ff_half, 1)
        return lax.dot_general(
            own, array, (((0,), (0,)), ((), ())), preferred_element_type=jnp.float32
        )

    total = count[0, 0] + count_other[0, 0]
    hessian = (2.0 / total * (outer(hidden) + outer(hidden_other)))[None]
    high, low = mix_table(routes, mixing, experts, part)
    mixed = jnp.dot(jnp.concatenate([high, low]), returned, preferred_element_type=jnp.float32)
    mixed = (mixed[:tok_rows] + mixed[tok_rows:]).astype(jnp.bfloat16)
    return mixed, hessian


def solution(mesh):
    placed = (
        P("expert", "token"),
        P("expert", None),
        P("expert", None),
        P("expert", None, "token"),
        P("expert", None, "token"),
        P("expert", None, "token"),
    )
    return jax.shard_map(
        shards,
        mesh=mesh,
        in_specs=placed,
        out_specs=(P("expert", "token"), P("expert", "token", None)),
        check_vma=False,
    )
```

```python
import functools

import jax
import jax.numpy as jnp
from jax import lax
from jax.experimental import pallas as pl
from jax.experimental.pallas import tpu as pltpu
from jax.sharding import PartitionSpec as P

EMPTY = 64.0
LOOKAHEAD = 4
VMEM_LIMIT = 61 * 1024 * 1024


def route_kernel(experts, part, wide, routes_hbm, tokens_hbm, out_hbm, routes_ref, tokens_ref, out, sems):
    tok_rows, half = tokens_ref.shape
    steps = half // wide
    load_routes = pltpu.make_async_copy(routes_hbm, routes_ref, sems.at[2 * steps])
    load_tokens = pltpu.make_async_copy(tokens_hbm, tokens_ref, sems.at[2 * steps + 1])
    load_routes.start()
    load_tokens.start()
    load_routes.wait()
    names = lax.broadcasted_iota(jnp.int32, (experts, tok_rows), 0)
    chosen = names == routes_ref[0:1, :]
    for k in range(1, routes_ref.shape[0]):
        chosen = chosen | (names == routes_ref[k : k + 1, :])
    first = lax.broadcasted_iota(jnp.int32, (tok_rows, tok_rows), 0)
    second = lax.broadcasted_iota(jnp.int32, (tok_rows, tok_rows), 1)
    rank = jnp.dot(
        chosen.astype(jnp.bfloat16), (first < second).astype(jnp.bfloat16),
        preferred_element_type=jnp.float32,
    )
    key = jnp.where(chosen, rank, -1.0)
    ones = jnp.ones((tok_rows, 128), jnp.bfloat16)
    group = experts // 2
    rows = group * 2 * part
    lane = lax.broadcasted_iota(jnp.int32, (rows, wide), 1)
    slot = lax.broadcasted_iota(jnp.int32, (group, 2 * part, tok_rows), 1).astype(jnp.float32)
    load_tokens.wait()
    copies = []
    for c in range(2):
        place = jnp.where(key[c * group : (c + 1) * group, None, :] == slot, 1.0, 0.0)
        place = place.reshape(rows, tok_rows).astype(jnp.bfloat16)
        taken = jnp.dot(place, ones, preferred_element_type=jnp.float32)[:, :1]
        for n in range(steps):
            columns = pl.ds(n * wide, wide)
            picked = jnp.dot(place, tokens_ref[:, columns], preferred_element_type=jnp.float32)
            if n == 0:
                picked = picked + jnp.where(lane == 0, EMPTY * (1.0 - taken), 0.0)
            spot = pl.ds(c * rows, rows)
            out[spot, columns] = picked.astype(out.dtype)
            copy = pltpu.make_async_copy(
                out.at[spot, columns], out_hbm.at[spot, columns], sems.at[c * steps + n]
            )
            copy.start()
            copies.append(copy)
    for copy in copies:
        copy.wait()


def place_rows(routes, tokens, experts, part):
    tok_rows, half = tokens.shape
    shape = (2 * experts * part, half)
    wide = 256
    return pl.pallas_call(
        functools.partial(route_kernel, experts, part, wide),
        out_shape=jax.ShapeDtypeStruct(shape, jnp.bfloat16),
        in_specs=[pl.BlockSpec(memory_space=pltpu.HBM)] * 2,
        out_specs=pl.BlockSpec(memory_space=pltpu.HBM),
        scratch_shapes=[
            pltpu.VMEM(routes.shape, routes.dtype),
            pltpu.VMEM(tokens.shape, tokens.dtype),
            pltpu.VMEM(shape, jnp.bfloat16),
            pltpu.SemaphoreType.DMA((2 * (half // wide) + 2,)),
        ],
        compiler_params=pltpu.CompilerParams(vmem_limit_bytes=VMEM_LIMIT),
    )(routes, tokens)


def expert_kernel(
    x_hbm, gate_own, up_own, gate_other, up_other, down_own, down_other,
    out_hbm, hid_hbm, count_hbm, x, first, second, outs, hid_ref, count_ref,
    x_sems, f_sems, s_sems, o_sems, e_sems,
):
    core = lax.axis_index("token")
    _, groups, part, half = x.shape
    rows = groups * part
    ff_half = gate_own.shape[2]
    wide = 256

    def load_x(f):
        return pltpu.make_async_copy(x_hbm.at[:, f], x.at[f], x_sems.at[f])

    def load_first(i, src, f):
        return pltpu.make_async_copy(
            src.at[0, pl.ds(f * half, half)], first.at[i, f], f_sems.at[2 * i + f]
        )

    queue = []
    cut = 768
    for i, src in enumerate((gate_own, up_own, gate_other, up_other)):
        for f in range(2):
            if i == 0 and f == 0:
                for n, span in enumerate((pl.ds(0, cut), pl.ds(cut, half - cut))):
                    queue.append(
                        pltpu.make_async_copy(
                            x_hbm.at[:, 0, :, span], x.at[0, :, :, span], x_sems.at[2 * n]
                        )
                    )
                    queue.append(
                        pltpu.make_async_copy(
                            src.at[0, span], first.at[0, 0, span], f_sems.at[8 * n]
                        )
                    )
                continue
            if i == 0:
                queue.append(load_x(f))
            queue.append(load_first(i, src, f))
    for i, src in enumerate((down_own, down_other)):
        queue.append(pltpu.make_async_copy(src.at[0], second.at[i], s_sems.at[i]))
    started = []

    def ahead(count):
        while len(started) < min(count, len(queue)):
            copy = queue[len(started)]
            copy.start()
            started.append(copy)

    done = []

    def ready(count):
        while len(done) < count:
            queue[len(done)].wait()
            done.append(None)
            ahead(len(done) + LOOKAHEAD)

    ahead(LOOKAHEAD)

    def features(f):
        return x[f].reshape(rows, half)

    def product(i):
        return jnp.dot(
            features(0), first[i, 0], preferred_element_type=jnp.float32
        ) + jnp.dot(features(1), first[i, 1], preferred_element_type=jnp.float32)

    def keep(side, gate, upper):
        hidden = jnp.where(valid, gate / (1.0 + jnp.exp(-gate)) * upper, 0.0)
        base = (core if side == 0 else 1 - core) * ff_half
        hid_ref[:, pl.ds(pl.multiple_of(base, ff_half), ff_half)] = hidden.astype(hid_ref.dtype)

    ready(2)
    gate = jnp.dot(
        x[0, :, :, :cut].reshape(rows, cut), first[0, 0, :cut], preferred_element_type=jnp.float32
    )
    ready(4)
    gate = gate + jnp.dot(
        x[0, :, :, cut:].reshape(rows, half - cut), first[0, 0, cut:],
        preferred_element_type=jnp.float32,
    )
    ready(6)
    gate = gate + jnp.dot(features(1), first[0, 1], preferred_element_type=jnp.float32)
    valid = x[0, :, :, :128].astype(jnp.float32).reshape(rows, 128)[:, :1] < EMPTY / 2
    count_ref[...] = jnp.full(count_ref.shape, jnp.sum(valid.astype(jnp.float32)))
    copies = [pltpu.make_async_copy(count_ref, count_hbm, e_sems.at[0])]
    copies[0].start()
    ready(8)
    upper = product(1)
    ready(10)
    keep(0, gate, upper)
    gate = product(2)
    ready(12)
    keep(1, gate, product(3))
    copies.append(pltpu.make_async_copy(hid_ref, hid_hbm, e_sems.at[1]))
    copies[1].start()
    for side in range(2):
        ready(13 + side)
        target = core if side == 0 else 1 - core
        for n in range(half // wide):
            columns = pl.ds(n * wide, wide)
            result = jnp.dot(
                hid_ref[...], second[side, :, columns], preferred_element_type=jnp.float32
            )
            outs[side, :, :, columns] = result.reshape(groups, part, wide).astype(outs.dtype)
            copy = pltpu.make_async_copy(
                outs.at[side, :, :, columns], out_hbm.at[:, target, :, columns],
                o_sems.at[side * (half // wide) + n],
            )
            copy.start()
            copies.append(copy)
    for copy in copies:
        copy.wait()


def run_experts(x, gate_own, up_own, gate_other, up_other, down_own, down_other):
    groups, _, part, half = x.shape
    rows = groups * part
    width = 2 * half
    ff_half = gate_own.shape[2]
    ff = 2 * ff_half
    far = pl.BlockSpec(memory_space=pltpu.HBM)
    return pl.pallas_call(
        expert_kernel,
        out_shape=(
            jax.ShapeDtypeStruct((groups, 2, part, half), jnp.bfloat16),
            jax.ShapeDtypeStruct((rows, ff), jnp.bfloat16),
            jax.ShapeDtypeStruct((8, 128), jnp.float32),
        ),
        in_specs=[far] * 7,
        out_specs=(far, far, far),
        scratch_shapes=[
            pltpu.VMEM((2, groups, part, half), jnp.bfloat16),
            pltpu.VMEM((4, 2, half, ff_half), jnp.bfloat16),
            pltpu.VMEM((2, ff, half), jnp.bfloat16),
            pltpu.VMEM((2, groups, part, half), jnp.bfloat16),
            pltpu.VMEM((rows, ff), jnp.bfloat16),
            pltpu.VMEM((8, 128), jnp.float32),
            pltpu.SemaphoreType.DMA((3,)),
            pltpu.SemaphoreType.DMA((9,)),
            pltpu.SemaphoreType.DMA((2,)),
            pltpu.SemaphoreType.DMA((2 * (half // 256),)),
            pltpu.SemaphoreType.DMA((2,)),
        ],
        compiler_params=pltpu.CompilerParams(vmem_limit_bytes=VMEM_LIMIT),
        cost_estimate=pl.CostEstimate(
            flops=2 * rows * width * ff * 3, bytes_accessed=6 * width * ff + 4 * rows * width,
            transcendentals=rows * ff,
        ),
    )(x, gate_own, up_own, gate_other, up_other, down_own, down_other)


def swap(array):
    return lax.ppermute(array, "token", [(0, 1), (1, 0)])


def mix_table(routes, mixing, experts, part):
    tok_rows = routes.shape[0]
    names = jnp.arange(experts, dtype=jnp.int32)
    match = routes[:, :, None] == names[None, None, :]
    chosen = jnp.any(match, axis=1)
    weight = jnp.sum(jnp.where(match, mixing[:, :, None], 0.0), axis=1)
    spots = jnp.arange(tok_rows, dtype=jnp.int32)
    before = (spots[:, None] > spots[None, :]).astype(jnp.bfloat16)
    rank = jnp.dot(before, chosen.astype(jnp.bfloat16), preferred_element_type=jnp.float32)
    key = jnp.where(chosen, rank.astype(jnp.int32), -1)
    slot = jnp.arange(2 * part, dtype=jnp.int32)
    place = key[:, :, None] == slot
    mixes = jnp.where(place, weight[:, :, None], 0.0).reshape(tok_rows, -1)
    high = lax.reduce_precision(mixes, 8, 7)
    return high.astype(jnp.bfloat16), (mixes - high).astype(jnp.bfloat16)


def shards(tokens, routes, mixing, gate_weight, up_weight, down_weight):
    tok_rows, half = tokens.shape
    experts = lax.axis_size("expert")
    capacity = 2 * tok_rows * routes.shape[1] // experts
    part = capacity // 2
    core = lax.axis_index("token")
    outgoing = place_rows(routes.T, tokens, experts, part).reshape(2 * experts, part, half)
    received = lax.all_to_all(outgoing, ("expert", "token"), 0, 0, tiled=True)
    x = received.reshape(experts, 2, part, half)
    gate_other, up_other, down_other = swap(gate_weight), swap(up_weight), swap(down_weight)
    out, hidden, count = run_experts(
        x, gate_weight, up_weight, gate_other, up_other, down_weight, down_other
    )
    returned = lax.all_to_all(
        out.reshape(2 * experts, part, half), ("expert", "token"), 0, 0, tiled=True
    ).reshape(-1, half)
    hidden_other, count_other = swap(hidden), swap(count)
    ff_half = gate_weight.shape[2]

    def outer(array):
        own = lax.dynamic_slice_in_dim(array, core * ff_half, ff_half, 1)
        return lax.dot_general(
            own, array, (((0,), (0,)), ((), ())), preferred_element_type=jnp.float32
        )

    total = count[0, 0] + count_other[0, 0]
    hessian = (2.0 / total * (outer(hidden) + outer(hidden_other)))[None]
    high, low = mix_table(routes, mixing, experts, part)
    mixed = jnp.dot(jnp.concatenate([high, low]), returned, preferred_element_type=jnp.float32)
    mixed = (mixed[:tok_rows] + mixed[tok_rows:]).astype(jnp.bfloat16)
    return mixed, hessian


def solution(mesh):
    placed = (
        P("expert", "token"),
        P("expert", None),
        P("expert", None),
        P("expert", None, "token"),
        P("expert", None, "token"),
        P("expert", None, "token"),
    )
    return jax.shard_map(
        shards,
        mesh=mesh,
        in_specs=placed,
        out_specs=(P("expert", "token"), P("expert", "token", None)),
        check_vma=False,
    )
```
